256 devices in a mesh: mem: 8 (over y, core), tile: 32 (over x, z).
Axes of the slice: x: 4, y: 4, z: 8, core: 2. Of those that a mesh axis runs over, the one named last changes fastest.
Arguments:
- atmos: float32 [64, 2048, 1024], P('mem', 'tile'), parts along dimension 0, may hold values from -6 to 6
- kappa: float32 [2048, 1024], P('tile'), may hold values from 0.02 to 0.24
- weights: bfloat16 [16384, 128, 128], P('tile'), may hold values from -0.5 to 0.5
- pair_land: int32 [16384], P('tile'), may hold values from 0 to 4095, as said below
- pair_atm: int32 [16384], P('tile'), may hold values from 0 to 511
- land_mask: int32 [4096], P('tile'), may hold values 0 or 1
Outputs:
- land: float32 [4096, 64, 128], P('tile', 'mem'), parts along dimension 1
The draws below stay inside these ranges and needn't reach their ends.
There are 8 independent parts, one for each index of `mem`. The reference program is written for one: setup_inputs(seed, part) draws one part's arguments, and reference() takes and returns one part's arrays. A program takes and returns all parts, laid end to end along the dimension named above; an argument that names none is the same for every part. Nothing has to cross between parts.
Inputs may be any that keep to these rules, and one draw needn't show every extreme that they name: `pair_land`: of the 512 pairs of one device, at most 32 write land blocks of any one device's range d * 128 to (d+1) * 128 - 1; one range, drawn from the seed, receives exactly 32 from every device.
All inputs are finite; a program needn't handle non-finite values. No bound on the sum of `land_mask` on one device may be relied on, other than what follows from the above.
Results may differ from the reference program's by a relative error of at most 0.0029.
Values sent between devices are 32-bit elements; how exact they have to be, the bound alone decides.
No kernel may reach another device: no remote copies, remote signals or barrier semaphores. Data moves between devices by JAX's collectives and lax.ppermute only.
A program may use at most 128 MiB of HBM per device.

```python
import math
import jax
import jax.numpy as jnp

FIELDS = 8
BLK = 128
COLS = 1024
PAIR_DEV = 512
LAND_DEV = 128
ROWS_ALL = 2048
ATM_BLK = 512
PAIRS = 16384
LAND_TOTAL = 4096
CAP = 32
N_TILE = 32


def draw_pair_land(key, part):
    key = jax.random.fold_in(key, 11)
    key_forced, key_rest = jax.random.split(key)
    required_pairs = jax.random.randint(key_forced, (), 0, N_TILE)
    owners = jnp.repeat(jnp.arange(N_TILE, dtype=jnp.int32), CAP)

    def one_device(sub):
        key_perm, key_local = jax.random.split(sub)
        scores = jax.random.permutation(key_perm, N_TILE * CAP).astype(jnp.int32)
        scores = jnp.where(owners == required_pairs, scores - N_TILE * CAP, scores)
        order = jnp.argsort(scores, stable=True)
        selected_tiles = owners[order][:PAIR_DEV]
        local = jax.random.randint(key_local, (PAIR_DEV,), 0, LAND_DEV)
        return selected_tiles * LAND_DEV + local
    return jax.vmap(one_device)(jax.random.split(key_rest, N_TILE)).reshape(-1).astype(jnp.int32)


def set_ends(drawn, key, low, top_value):
    longest = drawn.shape.index(max(drawn.shape))
    spots = []
    for shift in (0, 1):
        where = [jax.random.randint(jax.random.fold_in(key, axis), (), 0, length) for axis, length in enumerate(drawn.shape)]
        where[longest] = (where[longest] + shift) % drawn.shape[longest]
        spots.append(tuple(where))
    return drawn.at[spots[0]].set(low).at[spots[1]].set(top_value)


def block_scale(own_key, extent, shards, smallest, high):
    loudness = 1.0
    for axis_at, parts in shards:
        draws = jax.random.uniform(jax.random.fold_in(jax.random.fold_in(own_key, 6), axis_at), (parts,), jnp.float32, smallest / len(shards), high / len(shards))
        loudness = loudness * jnp.repeat(jnp.exp(draws), extent[axis_at] // parts).reshape((-1,) + (1,) * (len(extent) - 1 - axis_at))
    return loudness


def scatter_about(own_key, dims, deviation, bound, cuts=(), kind=jnp.bfloat16):
    values = jax.random.normal(own_key, dims, jnp.float32) * deviation
    if len(cuts) > 0:
        values = block_scale(own_key, dims, cuts, -0.22, 0.18) * values
    return jnp.clip(values, min=-bound, max=bound).astype(kind)


def setup_inputs(seed: int = 0, part: int = 0) -> dict:
    key_of = jax.random.split(jax.random.key(seed), 7)
    part_splits = jax.random.split(jax.random.fold_in(key_of[6], part), 7)
    return {
        "atmos": scatter_about(part_splits[0], (FIELDS, ROWS_ALL, COLS), 1.0, 6.0, ((1, 32),), jnp.float32),
        "kappa": jnp.clip(jnp.exp(math.log(0.24) - 2.4849066 * jax.random.uniform(key_of[1], (ROWS_ALL, COLS), jnp.float32) ** block_scale(key_of[1], (ROWS_ALL, COLS), ((0, 32),), -0.2, 0.2)), 0.02, 0.24),
        "weights": scatter_about(key_of[2], (PAIRS, BLK, BLK), BLK ** -0.5, 0.5, ((0, 32),)),
        "pair_land": draw_pair_land(jax.random.fold_in(key_of[6], 71), part),
        "pair_atm": set_ends(jax.random.randint(key_of[4], (PAIRS,), 0, ATM_BLK), jax.random.fold_in(key_of[4], 1), 0, ATM_BLK - 1).astype(jnp.int32),
        "land_mask": set_ends((jax.random.randint(key_of[5], (LAND_TOTAL,), 0, 4) < 3).astype(jnp.int32), jax.random.fold_in(key_of[5], 1), 0, 1),
    }


def reference(atmos, kappa, weights, pair_land, pair_atm, land_mask):
    padded = jnp.pad(atmos, ((0, 0), (1, 1), (0, 0)))
    north = padded[:, :-2, :]
    south = padded[:, 2:, :]
    east = jnp.roll(atmos, -1, axis=2)
    west = jnp.roll(atmos, 1, axis=2)
    smoothed = (atmos + kappa[None] * (north + south + east + west - 4.0 * atmos)).astype(jnp.bfloat16)
    blocks = smoothed.reshape(FIELDS, ROWS_ALL * COLS // BLK, BLK).transpose(1, 0, 2)
    owner = (jnp.arange(PAIRS, dtype=jnp.int32) // PAIR_DEV).astype(jnp.int32)
    index = (owner * ATM_BLK + pair_atm).astype(jnp.int32)
    selected_pairs = jnp.take(blocks, index, axis=0).astype(jnp.float32)
    remap_contribution_part = jnp.einsum("tuv,tvi->tui", selected_pairs, weights.astype(jnp.float32))
    summed = jax.ops.segment_sum(remap_contribution_part, pair_land, num_segments=LAND_TOTAL)
    return summed * land_mask.astype(jnp.float32)[:, None, None]
```

```python
import jax
import jax.numpy as jnp
from jax import lax
from jax.experimental import pallas as pl
from jax.experimental.pallas import tpu as pltpu
from jax.sharding import PartitionSpec as P

X, Z = 4, 8
F, B = 8, 128
ROWS, COLS = 64, 1024
LAND = 128
PAIRS = 512
CAP = 32
EMPTY = 2 * LAND
GROUP = 16
PART = 32
WEIGHT_PARTS = PAIRS // PART
FAR_VMEM, NEAR_VMEM = 56, 48
DISTANCES = (4, 3, 2, 1, 0)
SIZES = (CAP, 2 * CAP, 2 * CAP, 2 * CAP, CAP)
STARTS = tuple(X * (sum(SIZES[:n]) + n) for n in range(len(SIZES) + 1))
BITS = 9
LAND_BITS = 12


def shift(dx, dz):
    return [
        (x * Z + z, ((x + dx) % X) * Z + (z + dz) % Z) for x in range(X) for z in range(Z)
    ]


def send_x(a, dx):
    return lax.ppermute(a, "tile", shift(dx, 0))


def send_z(a, dz):
    return lax.ppermute(a, "tile", shift(0, dz))


def make_plan(packed, jobs_ref, order_ref, bounds_ref, table_ref):
    land, atm = packed & ((1 << LAND_BITS) - 1), packed >> LAND_BITS
    t = lax.axis_index("tile")
    x, z = t // Z, t % Z
    owner, row = land >> 7, land & (LAND - 1)
    ex = ((owner >> 3) - x) & (X - 1)
    delta = ((owner & (Z - 1)) - z) & (Z - 1)
    dist = jnp.minimum(delta, Z - delta)
    start = jnp.zeros_like(dist)
    for n, d in enumerate(DISTANCES):
        start = jnp.where(dist == d, STARTS[n] + ex * (SIZES[n] + 1), start)
    bounds_ref[0] = jnp.sum((start < STARTS[1]).astype(jnp.int32))
    target = row + jnp.where(delta > 4, LAND, 0) - EMPTY

    def column(a):
        return jnp.transpose(jnp.broadcast_to(a, (F, PAIRS)))[:, 0:1]

    def total(a):
        return jnp.sum(a, axis=0, keepdims=True)

    square = (PAIRS, PAIRS)
    p_row = lax.broadcasted_iota(jnp.int32, (1, PAIRS), 1)
    earlier = lax.broadcasted_iota(jnp.int32, square, 0) < lax.broadcasted_iota(
        jnp.int32, square, 1
    )
    start_col = column(start)
    one = jnp.ones(square, jnp.int32)
    nil = jnp.zeros(square, jnp.int32)
    rank = total(jnp.where((start_col == start) & earlier, one, nil))
    place = rank + total(jnp.where(start_col < start, one, nil))
    slot = start + rank
    job = p_row + (atm << BITS) + (slot << (2 * BITS))
    jobs_ref[...] = job
    order_ref[...] = total(jnp.where(column(place) == p_row, column(job), 0))
    slot_col, target_col = column(slot), column(target)
    lane = lax.broadcasted_iota(jnp.int32, (1, B), 1)
    for n in range(len(SIZES)):
        for m in range(X // 2):
            head = STARTS[n] + 2 * m * (SIZES[n] + 1)
            spot = jnp.where(lane < B // 2, head + lane, head + SIZES[n] + 1 + lane - B // 2)
            spot = jnp.where(lane % (B // 2) < SIZES[n], spot, -1)
            hit = total(jnp.where(slot_col == spot, target_col, 0))
            k = n * (X // 2) + m
            table_ref[k : k + 1] = (EMPTY + hit).astype(jnp.float32)


def start_weights(w_ref, w, sem):
    for n in range(WEIGHT_PARTS):
        at = pl.ds(n * PART, PART)
        pltpu.make_async_copy(w_ref.at[at], w.at[at], sem.at[n]).start()


def wait_weights(w_ref, w, sem, n):
    at = pl.ds(n * PART, PART)
    pltpu.make_async_copy(w_ref.at[at], w.at[at], sem.at[n]).wait()


def put_targets(table, send, first, last, base):
    for n in range(first, last):
        for e in range(X):
            end = STARTS[n] + (e + 1) * (SIZES[n] + 1) - 1 - base
            k = n * (X // 2) + e // 2
            send[end, 0:1] = table[k : k + 1]


def put_messages(send, outs, sem, first, last, base):
    copies = []
    for n in range(first, last):
        for e in range(X):
            at = STARTS[n] + e * (SIZES[n] + 1) - base
            k = len(copies)
            copies.append(
                pltpu.make_async_copy(send.at[pl.ds(at, SIZES[n] + 1)], outs[k], sem.at[k])
            )
    for c in copies:
        c.start()
    for c in copies:
        c.wait()


def far_kernel(
    atmos, kappa, packed, north, south, w_ref, smooth, jobs, table, *rest
):
    *outs, field, coeff, pairs, edge, rows, order, place, bounds, w, send, w_sem, out_sem, sem = rest
    per = COLS // B
    small = pltpu.make_async_copy(packed, pairs, sem.at[per])
    small.start()
    copies = [
        pltpu.make_async_copy(atmos.at[:, pl.ds(c * B, B)], field.at[c], sem.at[c])
        for c in range(per)
    ] + [
        pltpu.make_async_copy(kappa, coeff, sem.at[per + 1]),
        pltpu.make_async_copy(north, edge.at[0], sem.at[per + 2]),
        pltpu.make_async_copy(south, edge.at[1], sem.at[per + 3]),
    ]
    for c in copies:
        c.start()
    start_weights(w_ref, w, w_sem)
    small.wait()
    make_plan(pairs[...], jobs, order, bounds, table)
    to_smem = pltpu.make_async_copy(order, place, sem.at[per])
    to_smem.start()
    for c in copies:
        c.wait()
    tile = lax.axis_index("tile")
    above = jnp.where(tile > 0, edge[0], 0.0)
    under = jnp.where(tile < X * Z - 1, edge[1], 0.0)

    def row(r):
        return jnp.concatenate([field[c, pl.ds(r, F, stride=ROWS), :] for c in range(per)], axis=1)

    def step(r, carry):
        prev, cur = carry
        nxt = row(jnp.minimum(r + 1, ROWS - 1))
        below = jnp.where(r < ROWS - 1, nxt, under)
        east = pltpu.roll(cur, COLS - 1, 1)
        west = pltpu.roll(cur, 1, 1)
        value = cur + coeff[pl.ds(r, 1), :] * (prev + below + east + west - 4.0 * cur)
        for c in range(per):
            rows[r * per + c] = value[:, c * B : (c + 1) * B]
        return cur, nxt

    lax.fori_loop(0, ROWS, step, (above, row(0)), unroll=2)
    save = pltpu.make_async_copy(rows, smooth, sem.at[0])
    save.start()
    put_targets(table, send, 0, 1, 0)
    to_smem.wait()
    for n in range(WEIGHT_PARTS):
        wait_weights(w_ref, w, w_sem, n)
    mask = (1 << BITS) - 1
    high = bounds[0]

    def multiply(n, carry):
        for j in range(GROUP):
            job = place[0, jnp.minimum(n * GROUP + j, high - 1)]
            block = rows[(job >> BITS) & mask].astype(jnp.bfloat16)
            send[job >> (2 * BITS)] = jnp.dot(
                block, w[job & mask], preferred_element_type=jnp.float32
            )
        return carry

    lax.fori_loop(0, (high + GROUP - 1) // GROUP, multiply, 0)
    put_messages(send, outs, out_sem, 0, 1, 0)
    save.wait()


def near_kernel(jobs, table, smooth, w_ref, *rest):
    *outs, rows, w, send, w_sem, out_sem, sem = rest
    base = STARTS[1] - 1
    start_weights(w_ref, w, w_sem)
    load = pltpu.make_async_copy(smooth, rows, sem)
    load.start()
    put_targets(table, send, 1, len(SIZES), base)
    load.wait()
    mask = (1 << BITS) - 1

    def multiply(n, carry):
        wait_weights(w_ref, w, w_sem, n)
        for j in range(PART):
            p = n * PART + j
            job = jobs[0, p]
            block = rows[(job >> BITS) & mask].astype(jnp.bfloat16)
            send[jnp.maximum((job >> (2 * BITS)) - base, 0)] = jnp.dot(
                block, w[p], preferred_element_type=jnp.float32
            )
        return carry

    lax.fori_loop(0, WEIGHT_PARTS, multiply, 0)
    put_messages(send, outs, out_sem, 1, len(SIZES), base)


def messages(first, last):
    return [
        jax.ShapeDtypeStruct((SIZES[n] + 1, F, B), jnp.float32)
        for n in range(first, last)
        for _ in range(X)
    ]


def remap_far(atmos, kappa, packed, north, south, weights):
    vmem, anywhere = (pl.BlockSpec(memory_space=m) for m in (pltpu.VMEM, pl.ANY))
    shapes = messages(0, 1)
    smooth, jobs, table, *outs = pl.pallas_call(
        far_kernel,
        out_shape=[
            jax.ShapeDtypeStruct((ROWS * COLS // B, F, B), jnp.float32),
            jax.ShapeDtypeStruct((1, PAIRS), jnp.int32),
            jax.ShapeDtypeStruct((len(SIZES) * X // 2, B), jnp.float32),
        ]
        + shapes,
        in_specs=[anywhere] * 6,
        out_specs=[anywhere, vmem, vmem] + [anywhere] * len(shapes),
        scratch_shapes=[
            pltpu.VMEM((COLS // B, F * ROWS, B), jnp.float32),
            pltpu.VMEM((ROWS, COLS), jnp.float32),
            pltpu.VMEM((1, PAIRS), jnp.int32),
            pltpu.VMEM((2, F, COLS), jnp.float32),
            pltpu.VMEM((ROWS * COLS // B, F, B), jnp.float32),
            pltpu.VMEM((1, PAIRS), jnp.int32),
            pltpu.SMEM((1, PAIRS), jnp.int32),
            pltpu.SMEM((1,), jnp.int32),
            pltpu.VMEM((PAIRS, B, B), jnp.bfloat16),
            pltpu.VMEM((STARTS[1], F, B), jnp.float32),
            pltpu.SemaphoreType.DMA((WEIGHT_PARTS,)),
            pltpu.SemaphoreType.DMA((len(shapes),)),
            pltpu.SemaphoreType.DMA((COLS // B + 4,)),
        ],
        compiler_params=pltpu.CompilerParams(vmem_limit_bytes=FAR_VMEM << 20),
        cost_estimate=pl.CostEstimate(flops=1 << 20, bytes_accessed=20 << 20, transcendentals=0),
    )(atmos.reshape(F * ROWS, COLS), kappa, packed, north, south, weights)
    return smooth, jobs, table, outs


def remap_near(jobs, table, smooth, weights):
    smem, vmem, anywhere = (
        pl.BlockSpec(memory_space=m) for m in (pltpu.SMEM, pltpu.VMEM, pl.ANY)
    )
    shapes = messages(1, len(SIZES))
    return pl.pallas_call(
        near_kernel,
        out_shape=shapes,
        in_specs=[smem, vmem, anywhere, anywhere],
        out_specs=[anywhere] * len(shapes),
        scratch_shapes=[
            pltpu.VMEM((ROWS * COLS // B, F, B), jnp.float32),
            pltpu.VMEM((PAIRS, B, B), jnp.bfloat16),
            pltpu.VMEM((STARTS[-1] - STARTS[1] + 1, F, B), jnp.float32),
            pltpu.SemaphoreType.DMA((WEIGHT_PARTS,)),
            pltpu.SemaphoreType.DMA((len(shapes),)),
            pltpu.SemaphoreType.DMA,
        ],
        compiler_params=pltpu.CompilerParams(vmem_limit_bytes=NEAR_VMEM << 20),
        cost_estimate=pl.CostEstimate(flops=1 << 20, bytes_accessed=24 << 20, transcendentals=0),
    )(jobs, table, smooth, weights)


def gather_kernel(size, a0, a1, a2, a3, out, wide, index, sem):
    for n, a in enumerate((a0, a1, a2, a3)):
        wide[n : n + 1] = a[size, 0:1].astype(jnp.int32)
    copy = pltpu.make_async_copy(wide, index, sem)
    copy.start()
    out[...] = jnp.zeros_like(out)
    copy.wait()
    for n, a in enumerate((a0, a1, a2, a3)):

        def add(s, carry, n=n, a=a):
            out[index[n, s + (n % 2) * (B // 2)]] += a[s]
            return carry

        lax.fori_loop(0, size, add, 0, unroll=8)


def gather_class(size, slots):
    return pl.pallas_call(
        lambda *refs: gather_kernel(size, *refs),
        out_shape=jax.ShapeDtypeStruct((EMPTY + 8, F, B), jnp.float32),
        in_specs=[pl.BlockSpec(memory_space=pltpu.VMEM)] * X,
        out_specs=pl.BlockSpec(memory_space=pltpu.VMEM),
        scratch_shapes=[
            pltpu.VMEM((F, B), jnp.int32),
            pltpu.SMEM((F, B), jnp.int32),
            pltpu.SemaphoreType.DMA,
        ],
        compiler_params=pltpu.CompilerParams(vmem_limit_bytes=2 << 20),
        cost_estimate=pl.CostEstimate(
            flops=1 << 32, bytes_accessed=1 << 20, transcendentals=0
        ),
    )(*slots)


def body(atmos, kappa, weights, pair_land, pair_atm, land_mask):
    tiles = X * Z
    north = lax.ppermute(atmos[:, -1, :], "tile", [(i, (i + 1) % tiles) for i in range(tiles)])
    south = lax.ppermute(atmos[:, 0, :], "tile", [((i + 1) % tiles, i) for i in range(tiles)])
    packed = (pair_land + (pair_atm << LAND_BITS)).reshape(1, PAIRS)
    smooth, jobs, table, out = remap_far(atmos, kappa, packed, north, south, weights)
    near = remap_near(jobs, table, smooth, weights)
    sends = [out] + [near[n * X : (n + 1) * X] for n in range(len(SIZES) - 1)]
    dense = {}
    came = None
    for n, (own, *away) in enumerate(sends):
        if came is not None:
            came, away = zip(*(lax.optimization_barrier(both) for both in zip(came, away)))
            dense[DISTANCES[n - 1]] = gather_class(SIZES[n - 1], [mine, *came])
        came, mine = [send_x(a, ex + 1) for ex, a in enumerate(away)], own
    dense[0] = gather_class(SIZES[-1], [mine, *came])
    half = LAND // 2
    pad = ((0, half), (0, 0), (0, 0))
    plus, minus = send_z(dense[4][:half], 1), send_z(dense[4][half:LAND], -1)
    plus, minus = jnp.pad(plus, pad), jnp.pad(minus, (pad[0][::-1], pad[1], pad[2]))
    for k in (3, 2, 1):
        plus = send_z(dense[k][:LAND] + plus, 1)
        minus = send_z(dense[k][LAND : 2 * LAND] + minus, -1)
    total = dense[0][:LAND] + plus + minus
    return total * land_mask.astype(jnp.float32)[:, None, None]


def solution(mesh):
    in_specs = (
        P("mem", "tile", None),
        P("tile", None),
        P("tile", None, None),
        P("tile"),
        P("tile"),
        P("tile"),
    )
    out_specs = P("tile", "mem", None)
    return jax.shard_map(body, mesh=mesh, in_specs=in_specs, out_specs=out_specs, check_vma=False)
```

```python
import jax
import jax.numpy as jnp
from jax import lax
from jax.experimental import pallas as pl
from jax.experimental.pallas import tpu as pltpu
from jax.sharding import PartitionSpec as P

X, Z = 4, 8
F, B = 8, 128
ROWS, COLS = 64, 1024
LAND = 128
PAIRS = 512
CAP = 32
EMPTY = 2 * LAND
GROUP = 16
PART = 32
WEIGHT_PARTS = PAIRS // PART
FAR_VMEM, NEAR_VMEM = 44, 44
DISTANCES = (4, 3, 2, 1, 0)
SIZES = (CAP, 2 * CAP, 2 * CAP, 2 * CAP, CAP)
STARTS = tuple(X * (sum(SIZES[:n]) + n) for n in range(len(SIZES) + 1))
BITS = 9
MESSAGES = X * len(SIZES)
META_ROWS = 1 + MESSAGES // 4
FAR = 2
LAND_BITS = 12


def shift(dx, dz):
    return [
        (x * Z + z, ((x + dx) % X) * Z + (z + dz) % Z) for x in range(X) for z in range(Z)
    ]


def send_x(a, dx):
    return lax.ppermute(a, "tile", shift(dx, 0))


def send_z(a, dz):
    return lax.ppermute(a, "tile", shift(0, dz))


def make_plan(packed, meta_ref, order_ref, bounds_ref, table_ref):
    land, atm = packed & ((1 << LAND_BITS) - 1), packed >> LAND_BITS
    t = lax.axis_index("tile")
    x, z = t // Z, t % Z
    owner, row = land >> 7, land & (LAND - 1)
    ex = ((owner >> 3) - x) & (X - 1)
    delta = ((owner & (Z - 1)) - z) & (Z - 1)
    dist = jnp.minimum(delta, Z - delta)
    start = jnp.zeros_like(dist)
    for n, d in enumerate(DISTANCES):
        start = jnp.where(dist == d, STARTS[n] + ex * (SIZES[n] + 1), start)
    bounds_ref[0] = jnp.sum((start < STARTS[FAR]).astype(jnp.int32))
    target = row + jnp.where(delta > 4, LAND, 0) - EMPTY

    def column(a):
        return jnp.transpose(jnp.broadcast_to(a, (F, PAIRS)))[:, 0:1]

    def total(a):
        return jnp.sum(a, axis=0, keepdims=True)

    square = (PAIRS, PAIRS)
    p_row = lax.broadcasted_iota(jnp.int32, (1, PAIRS), 1)
    earlier = lax.broadcasted_iota(jnp.int32, square, 0) < lax.broadcasted_iota(
        jnp.int32, square, 1
    )
    start_col = column(start)
    one = jnp.ones(square, jnp.int32)
    nil = jnp.zeros(square, jnp.int32)
    rank = total(jnp.where((start_col == start) & earlier, one, nil))
    place = rank + total(jnp.where(start_col < start, one, nil))
    slot = start + rank
    job = p_row + (atm << BITS) + (slot << (2 * BITS))
    meta_ref[0:1] = job
    order_ref[...] = total(jnp.where(column(place) == p_row, column(job), 0))
    slot_col, target_col = column(slot), column(target)
    lane = lax.broadcasted_iota(jnp.int32, (1, B), 1)
    for n in range(len(SIZES)):
        for m in range(X // 2):
            head = STARTS[n] + 2 * m * (SIZES[n] + 1)
            spot = jnp.where(lane < B // 2, head + lane, head + SIZES[n] + 1 + lane - B // 2)
            spot = jnp.where(lane % (B // 2) < SIZES[n], spot, -1)
            hit = total(jnp.where(slot_col == spot, target_col, 0))
            used = (hit != 0).astype(jnp.int32)
            left = jnp.sum(jnp.where(lane < B // 2, used, 0), axis=1, keepdims=True)
            right = jnp.sum(used, axis=1, keepdims=True) - left
            k = n * (X // 2) + m
            table_ref[k : k + 1] = EMPTY + hit
            table_ref[MESSAGES // 2 + k : MESSAGES // 2 + k + 1] = jnp.where(
                lane < B // 2, left, right
            )
    for k in range(MESSAGES):
        at = slice(k % 4 * B, (k % 4 + 1) * B)
        meta_ref[1 + k // 4 : 2 + k // 4, at] = table_ref[k : k + 1]


def start_weights(w_ref, w, sem):
    for n in range(WEIGHT_PARTS):
        at = pl.ds(n * PART, PART)
        pltpu.make_async_copy(w_ref.at[at], w.at[at], sem.at[n]).start()


def wait_weights(w_ref, w, sem, n):
    at = pl.ds(n * PART, PART)
    pltpu.make_async_copy(w_ref.at[at], w.at[at], sem.at[n]).wait()


def put_targets(row, send, first, last, base):
    for n in range(first, last):
        for e in range(X):
            end = STARTS[n] + (e + 1) * (SIZES[n] + 1) - 1 - base
            k = n * (X // 2) + e // 2
            send[end, 0:1] = row(k).astype(jnp.float32)
            send[end, 1:2] = row(MESSAGES // 2 + k).astype(jnp.float32)


def multiply_two(left, right, w):
    left, right = left.astype(jnp.bfloat16), right.astype(jnp.bfloat16)
    nil = jnp.zeros_like(left)
    both = jnp.concatenate(
        [jnp.concatenate([left, nil], axis=1), jnp.concatenate([nil, right], axis=1)], axis=0
    )
    out = jnp.dot(both, w, preferred_element_type=jnp.float32)
    return out[:F], out[F:]


def put_messages(send, outs, sem, first, last, base):
    copies = []
    for n in range(first, last):
        for e in range(X):
            at = STARTS[n] + e * (SIZES[n] + 1) - base
            k = len(copies)
            copies.append(
                pltpu.make_async_copy(send.at[pl.ds(at, SIZES[n] + 1)], outs[k], sem.at[k])
            )
    for c in copies:
        c.start()
    for c in copies:
        c.wait()


def far_kernel(atmos, kappa, packed, north, south, w_ref, smooth, meta, *rest):
    *outs, field, coeff, pairs, edge, rows, order, table, place, bounds, w, send = rest[:-3]
    w_sem, out_sem, sem = rest[-3:]
    per = COLS // B
    small = pltpu.make_async_copy(packed, pairs, sem.at[per])
    small.start()
    copies = [
        pltpu.make_async_copy(atmos.at[:, pl.ds(c * B, B)], field.at[c], sem.at[c])
        for c in range(per)
    ] + [
        pltpu.make_async_copy(kappa, coeff, sem.at[per + 1]),
        pltpu.make_async_copy(north, edge.at[0], sem.at[per + 2]),
        pltpu.make_async_copy(south, edge.at[1], sem.at[per + 3]),
    ]
    for c in copies:
        c.start()
    small.wait()
    for c in copies:
        c.wait()
    start_weights(w_ref, w, w_sem)
    make_plan(pairs[...], meta, order, bounds, table)
    to_smem = pltpu.make_async_copy(order, place, sem.at[per])
    to_smem.start()
    tile = lax.axis_index("tile")
    above = jnp.where(tile > 0, edge[0], 0.0)
    under = jnp.where(tile < X * Z - 1, edge[1], 0.0)

    def row(r):
        return jnp.concatenate([field[c, pl.ds(r, F, stride=ROWS), :] for c in range(per)], axis=1)

    def step(r, carry):
        prev, cur = carry
        nxt = row(jnp.minimum(r + 1, ROWS - 1))
        below = jnp.where(r < ROWS - 1, nxt, under)
        east = pltpu.roll(cur, COLS - 1, 1)
        west = pltpu.roll(cur, 1, 1)
        value = cur + coeff[pl.ds(r, 1), :] * (prev + below + east + west - 4.0 * cur)
        for c in range(per):
            rows[r * per + c] = value[:, c * B : (c + 1) * B]
        return cur, nxt

    lax.fori_loop(0, ROWS, step, (above, row(0)), unroll=2)
    save = pltpu.make_async_copy(rows, smooth, sem.at[0])
    save.start()
    put_targets(lambda k: table[k : k + 1], send, 0, FAR, 0)
    to_smem.wait()
    for n in range(WEIGHT_PARTS):
        wait_weights(w_ref, w, w_sem, n)
    mask = (1 << BITS) - 1
    high = bounds[0]

    def multiply(n, carry):
        for j in range(0, GROUP, 2):
            one = place[0, jnp.minimum(n * GROUP + j, high - 1)]
            two = place[0, jnp.minimum(n * GROUP + j + 1, high - 1)]
            send[one >> (2 * BITS)], send[two >> (2 * BITS)] = multiply_two(
                rows[(one >> BITS) & mask],
                rows[(two >> BITS) & mask],
                jnp.concatenate([w[one & mask], w[two & mask]], axis=0),
            )
        return carry

    lax.fori_loop(0, (high + GROUP - 1) // GROUP, multiply, 0)
    put_messages(send, outs, out_sem, 0, FAR, 0)
    save.wait()


def near_kernel(meta, smooth, w_ref, *rest):
    *outs, info, jobs, rows, w, send, w_sem, out_sem, sem = rest
    base = STARTS[FAR] - 1
    loads = [
        pltpu.make_async_copy(meta, info, sem.at[0]),
        pltpu.make_async_copy(meta.at[pl.ds(0, 1)], jobs, sem.at[1]),
        pltpu.make_async_copy(smooth, rows, sem.at[2]),
    ]
    for c in loads:
        c.start()
    start_weights(w_ref, w, w_sem)
    for c in loads:
        c.wait()
    put_targets(
        lambda k: info[1 + k // 4 : 2 + k // 4, k % 4 * B : (k % 4 + 1) * B],
        send, FAR, len(SIZES), base,
    )
    mask = (1 << BITS) - 1

    def multiply(n, carry):
        wait_weights(w_ref, w, w_sem, n)
        for j in range(0, PART, 2):
            p = n * PART + j
            one, two = jobs[0, p], jobs[0, p + 1]
            to_one = jnp.maximum((one >> (2 * BITS)) - base, 0)
            to_two = jnp.maximum((two >> (2 * BITS)) - base, 0)
            send[to_one], send[to_two] = multiply_two(
                rows[(one >> BITS) & mask],
                rows[(two >> BITS) & mask],
                w[pl.ds(p, 2)].reshape(2 * B, B),
            )
        return carry

    lax.fori_loop(0, WEIGHT_PARTS, multiply, 0)
    put_messages(send, outs, out_sem, FAR, len(SIZES), base)


def messages(first, last):
    return [
        jax.ShapeDtypeStruct((SIZES[n] + 1, F, B), jnp.float32)
        for n in range(first, last)
        for _ in range(X)
    ]


def remap_far(atmos, kappa, packed, north, south, weights):
    vmem, anywhere = (pl.BlockSpec(memory_space=m) for m in (pltpu.VMEM, pl.ANY))
    shapes = messages(0, FAR)
    smooth, meta, *outs = pl.pallas_call(
        far_kernel,
        out_shape=[
            jax.ShapeDtypeStruct((ROWS * COLS // B, F, B), jnp.float32),
            jax.ShapeDtypeStruct((META_ROWS, PAIRS), jnp.int32),
        ]
        + shapes,
        in_specs=[anywhere] * 6,
        out_specs=[anywhere, vmem] + [anywhere] * len(shapes),
        scratch_shapes=[
            pltpu.VMEM((COLS // B, F * ROWS, B), jnp.float32),
            pltpu.VMEM((ROWS, COLS), jnp.float32),
            pltpu.VMEM((1, PAIRS), jnp.int32),
            pltpu.VMEM((2, F, COLS), jnp.float32),
            pltpu.VMEM((ROWS * COLS // B, F, B), jnp.float32),
            pltpu.VMEM((1, PAIRS), jnp.int32),
            pltpu.VMEM((MESSAGES, B), jnp.int32),
            pltpu.SMEM((1, PAIRS), jnp.int32),
            pltpu.SMEM((1,), jnp.int32),
            pltpu.VMEM((PAIRS, B, B), jnp.bfloat16),
            pltpu.VMEM((STARTS[FAR], F, B), jnp.float32),
            pltpu.SemaphoreType.DMA((WEIGHT_PARTS,)),
            pltpu.SemaphoreType.DMA((len(shapes),)),
            pltpu.SemaphoreType.DMA((COLS // B + 4,)),
        ],
        compiler_params=pltpu.CompilerParams(vmem_limit_bytes=FAR_VMEM << 20),
        cost_estimate=pl.CostEstimate(flops=1 << 20, bytes_accessed=20 << 20, transcendentals=0),
    )(atmos.reshape(F * ROWS, COLS), kappa, packed, north, south, weights)
    return smooth, meta, outs


def remap_near(meta, smooth, weights):
    shapes = messages(FAR, len(SIZES))
    return pl.pallas_call(
        near_kernel,
        out_shape=shapes,
        in_specs=[pl.BlockSpec(memory_space=pl.ANY)] * 3,
        out_specs=[pl.BlockSpec(memory_space=pl.ANY)] * len(shapes),
        scratch_shapes=[
            pltpu.VMEM((META_ROWS, PAIRS), jnp.int32),
            pltpu.SMEM((1, PAIRS), jnp.int32),
            pltpu.VMEM((ROWS * COLS // B, F, B), jnp.float32),
            pltpu.VMEM((PAIRS, B, B), jnp.bfloat16),
            pltpu.VMEM((STARTS[-1] - STARTS[FAR] + 1, F, B), jnp.float32),
            pltpu.SemaphoreType.DMA((WEIGHT_PARTS,)),
            pltpu.SemaphoreType.DMA((len(shapes),)),
            pltpu.SemaphoreType.DMA((3,)),
        ],
        compiler_params=pltpu.CompilerParams(vmem_limit_bytes=NEAR_VMEM << 20),
        cost_estimate=pl.CostEstimate(flops=1 << 33, bytes_accessed=24 << 20, transcendentals=0),
    )(meta, smooth, weights)


def gather_kernel(size, a0, a1, a2, a3, out, wide, index, sem):
    for n, a in enumerate((a0, a1, a2, a3)):
        wide[n : n + 1] = a[size, 0:1].astype(jnp.int32)
        wide[X + n : X + n + 1] = a[size, 1:2].astype(jnp.int32)
    copy = pltpu.make_async_copy(wide, index, sem)
    copy.start()
    out[...] = jnp.zeros_like(out)
    copy.wait()
    for n, a in enumerate((a0, a1, a2, a3)):

        lane = (n % 2) * (B // 2)

        def add(g, carry, n=n, a=a, lane=lane):
            for j in range(8):
                out[index[n, lane + g * 8 + j]] += a[g * 8 + j]
            return carry

        lax.fori_loop(0, (index[X + n, lane] + 7) // 8, add, 0)


def gather_class(size, slots):
    return pl.pallas_call(
        lambda *refs: gather_kernel(size, *refs),
        out_shape=jax.ShapeDtypeStruct((EMPTY + 8, F, B), jnp.float32),
        in_specs=[pl.BlockSpec(memory_space=pltpu.VMEM)] * X,
        out_specs=pl.BlockSpec(memory_space=pltpu.VMEM),
        scratch_shapes=[
            pltpu.VMEM((F, B), jnp.int32),
            pltpu.SMEM((F, B), jnp.int32),
            pltpu.SemaphoreType.DMA,
        ],
        compiler_params=pltpu.CompilerParams(vmem_limit_bytes=2 << 20),
        cost_estimate=pl.CostEstimate(
            flops=1 << 32, bytes_accessed=1 << 20, transcendentals=0
        ),
    )(*slots)


def body(atmos, kappa, weights, pair_land, pair_atm, land_mask):
    tiles = X * Z
    north = lax.ppermute(atmos[:, -1, :], "tile", [(i, (i + 1) % tiles) for i in range(tiles)])
    south = lax.ppermute(atmos[:, 0, :], "tile", [((i + 1) % tiles, i) for i in range(tiles)])
    packed = (pair_land + (pair_atm << LAND_BITS)).reshape(1, PAIRS)
    smooth, meta, far = remap_far(atmos, kappa, packed, north, south, weights)
    sends = [*far, *remap_near(meta, smooth, weights)]
    sends = [sends[n * X : (n + 1) * X] for n in range(len(SIZES))]
    dense = {}
    came = None
    for n, (own, *away) in enumerate(sends):
        if came is not None:
            if n >= FAR:
                came, away = zip(*(lax.optimization_barrier(both) for both in zip(came, away)))
            dense[DISTANCES[n - 1]] = gather_class(SIZES[n - 1], [mine, *came])
        came, mine = [send_x(a, ex + 1) for ex, a in enumerate(away)], own
    dense[0] = gather_class(SIZES[-1], [mine, *came])
    half = LAND // 2
    pad = ((0, half), (0, 0), (0, 0))
    plus, minus = send_z(dense[4][:half], 1), send_z(dense[4][half:LAND], -1)
    plus, minus = jnp.pad(plus, pad), jnp.pad(minus, (pad[0][::-1], pad[1], pad[2]))
    for k in (3, 2, 1):
        plus = send_z(dense[k][:LAND] + plus, 1)
        minus = send_z(dense[k][LAND : 2 * LAND] + minus, -1)
    total = dense[0][:LAND] + plus + minus
    return total * land_mask.astype(jnp.float32)[:, None, None]


def solution(mesh):
    in_specs = (
        P("mem", "tile", None),
        P("tile", None),
        P("tile", None, None),
        P("tile"),
        P("tile"),
        P("tile"),
    )
    out_specs = P("tile", "mem", None)
    return jax.shard_map(body, mesh=mesh, in_specs=in_specs, out_specs=out_specs, check_vma=False)
```

```python
import jax
import jax.numpy as jnp
from jax import lax
from jax.experimental import pallas as pl
from jax.experimental.pallas import tpu as pltpu
from jax.sharding import PartitionSpec as P

X, Z = 4, 8
F, B = 8, 128
ROWS, COLS = 64, 1024
LAND = 128
PAIRS = 512
CAP = 32
EMPTY = 2 * LAND
GROUP = 16
PART = 32
WEIGHT_PARTS = PAIRS // PART
FAR_VMEM, NEAR_VMEM = 50, 44
DISTANCES = (4, 3, 2, 1, 0)
SIZES = (CAP, 2 * CAP, 2 * CAP, 2 * CAP, CAP)
STARTS = tuple(X * (sum(SIZES[:n]) + n) for n in range(len(SIZES) + 1))
BITS = 9
MESSAGES = X * len(SIZES)
META_ROWS = 1 + MESSAGES // 4
FAR = 2
LAND_BITS = 12


def shift(dx, dz):
    return [
        (x * Z + z, ((x + dx) % X) * Z + (z + dz) % Z) for x in range(X) for z in range(Z)
    ]


def send_x(a, dx):
    return lax.ppermute(a, "tile", shift(dx, 0))


def send_z(a, dz):
    return lax.ppermute(a, "tile", shift(0, dz))


def make_plan(packed, meta_ref, order_ref, bounds_ref, table_ref):
    land, atm = packed & ((1 << LAND_BITS) - 1), packed >> LAND_BITS
    t = lax.axis_index("tile")
    x, z = t // Z, t % Z
    owner, row = land >> 7, land & (LAND - 1)
    ex = ((owner >> 3) - x) & (X - 1)
    delta = ((owner & (Z - 1)) - z) & (Z - 1)
    dist = jnp.minimum(delta, Z - delta)
    start = jnp.zeros_like(dist)
    for n, d in enumerate(DISTANCES):
        start = jnp.where(dist == d, STARTS[n] + ex * (SIZES[n] + 1), start)
    bounds_ref[0] = jnp.sum((start < STARTS[FAR]).astype(jnp.int32))
    target = row + jnp.where(delta > 4, LAND, 0) - EMPTY

    def column(a):
        return jnp.transpose(jnp.broadcast_to(a, (F, PAIRS)))[:, 0:1]

    def total(a):
        return jnp.sum(a, axis=0, keepdims=True)

    square = (PAIRS, PAIRS)
    p_row = lax.broadcasted_iota(jnp.int32, (1, PAIRS), 1)
    earlier = lax.broadcasted_iota(jnp.int32, square, 0) < lax.broadcasted_iota(
        jnp.int32, square, 1
    )
    start_col = column(start)
    one = jnp.ones(square, jnp.int32)
    nil = jnp.zeros(square, jnp.int32)
    rank = total(jnp.where((start_col == start) & earlier, one, nil))
    place = rank + total(jnp.where(start_col < start, one, nil))
    slot = start + rank
    job = p_row + (atm << BITS) + (slot << (2 * BITS))
    meta_ref[0:1] = job
    order_ref[...] = total(jnp.where(column(place) == p_row, column(job), 0))
    slot_col, target_col = column(slot), column(target)
    lane = lax.broadcasted_iota(jnp.int32, (1, B), 1)
    for n in range(len(SIZES)):
        for m in range(X // 2):
            head = STARTS[n] + 2 * m * (SIZES[n] + 1)
            spot = jnp.where(lane < B // 2, head + lane, head + SIZES[n] + 1 + lane - B // 2)
            spot = jnp.where(lane % (B // 2) < SIZES[n], spot, -1)
            hit = total(jnp.where(slot_col == spot, target_col, 0))
            used = (hit != 0).astype(jnp.int32)
            left = jnp.sum(jnp.where(lane < B // 2, used, 0), axis=1, keepdims=True)
            right = jnp.sum(used, axis=1, keepdims=True) - left
            k = n * (X // 2) + m
            table_ref[k : k + 1] = EMPTY + hit
            table_ref[MESSAGES // 2 + k : MESSAGES // 2 + k + 1] = jnp.where(
                lane < B // 2, left, right
            )
    for k in range(MESSAGES):
        at = slice(k % 4 * B, (k % 4 + 1) * B)
        meta_ref[1 + k // 4 : 2 + k // 4, at] = table_ref[k : k + 1]


def start_weights(w_ref, w, sem):
    for n in range(WEIGHT_PARTS):
        at = pl.ds(n * PART, PART)
        pltpu.make_async_copy(w_ref.at[at], w.at[at], sem.at[n]).start()


def wait_weights(w_ref, w, sem, n):
    at = pl.ds(n * PART, PART)
    pltpu.make_async_copy(w_ref.at[at], w.at[at], sem.at[n]).wait()


def put_targets(row, send, first, last, base):
    for n in range(first, last):
        for e in range(X):
            end = STARTS[n] + (e + 1) * (SIZES[n] + 1) - 1 - base
            k = n * (X // 2) + e // 2
            send[end, 0:1] = row(k).astype(jnp.float32)
            send[end, 1:2] = row(MESSAGES // 2 + k).astype(jnp.float32)


def multiply_two(left, right, w):
    left, right = left.astype(jnp.bfloat16), right.astype(jnp.bfloat16)
    nil = jnp.zeros_like(left)
    both = jnp.concatenate(
        [jnp.concatenate([left, nil], axis=1), jnp.concatenate([nil, right], axis=1)], axis=0
    )
    out = jnp.dot(both, w, preferred_element_type=jnp.float32)
    return out[:F], out[F:]


def put_messages(send, outs, sem, first, last, base):
    copies = []
    for n in range(first, last):
        for e in range(X):
            at = STARTS[n] + e * (SIZES[n] + 1) - base
            k = len(copies)
            copies.append(
                pltpu.make_async_copy(send.at[pl.ds(at, SIZES[n] + 1)], outs[k], sem.at[k])
            )
    for c in copies:
        c.start()
    for c in copies:
        c.wait()


def far_kernel(atmos, kappa, packed, north, south, w_ref, smooth, meta, *rest):
    *outs, field, coeff, pairs, edge, rows, order, table, place, bounds, w, send = rest[:-3]
    w_sem, out_sem, sem = rest[-3:]
    per = COLS // B
    small = pltpu.make_async_copy(packed, pairs, sem.at[per])
    small.start()
    copies = [
        pltpu.make_async_copy(atmos.at[:, pl.ds(c * B, B)], field.at[c], sem.at[c])
        for c in range(per)
    ] + [
        pltpu.make_async_copy(kappa, coeff, sem.at[per + 1]),
        pltpu.make_async_copy(north, edge.at[0], sem.at[per + 2]),
        pltpu.make_async_copy(south, edge.at[1], sem.at[per + 3]),
    ]
    for c in copies:
        c.start()
    small.wait()
    for c in copies:
        c.wait()
    start_weights(w_ref, w, w_sem)
    make_plan(pairs[...], meta, order, bounds, table)
    to_smem = pltpu.make_async_copy(order, place, sem.at[per])
    to_smem.start()
    tile = lax.axis_index("tile")
    above = jnp.where(tile > 0, edge[0], 0.0)
    under = jnp.where(tile < X * Z - 1, edge[1], 0.0)

    def row(r):
        return jnp.concatenate([field[c, pl.ds(r, F, stride=ROWS), :] for c in range(per)], axis=1)

    def step(r, carry):
        prev, cur = carry
        nxt = row(jnp.minimum(r + 1, ROWS - 1))
        below = jnp.where(r < ROWS - 1, nxt, under)
        east = pltpu.roll(cur, COLS - 1, 1)
        west = pltpu.roll(cur, 1, 1)
        value = cur + coeff[pl.ds(r, 1), :] * (prev + below + east + west - 4.0 * cur)
        for c in range(per):
            rows[r * per + c] = value[:, c * B : (c + 1) * B]
        return cur, nxt

    lax.fori_loop(0, ROWS, step, (above, row(0)), unroll=4)
    save = pltpu.make_async_copy(rows, smooth, sem.at[0])
    save.start()
    put_targets(lambda k: table[k : k + 1], send, 0, FAR, 0)
    to_smem.wait()
    for n in range(WEIGHT_PARTS):
        wait_weights(w_ref, w, w_sem, n)
    mask = (1 << BITS) - 1
    high = bounds[0]

    def multiply(n, carry):
        for j in range(0, GROUP, 2):
            one = place[0, jnp.minimum(n * GROUP + j, high - 1)]
            two = place[0, jnp.minimum(n * GROUP + j + 1, high - 1)]
            send[one >> (2 * BITS)], send[two >> (2 * BITS)] = multiply_two(
                rows[(one >> BITS) & mask],
                rows[(two >> BITS) & mask],
                jnp.concatenate([w[one & mask], w[two & mask]], axis=0),
            )
        return carry

    lax.fori_loop(0, (high + GROUP - 1) // GROUP, multiply, 0)
    put_messages(send, outs, out_sem, 0, FAR, 0)
    save.wait()


def near_kernel(meta, smooth, w_ref, *rest):
    *outs, info, jobs, rows, w, send, w_sem, out_sem, sem = rest
    base = STARTS[FAR] - 1
    loads = [
        pltpu.make_async_copy(meta, info, sem.at[0]),
        pltpu.make_async_copy(meta.at[pl.ds(0, 1)], jobs, sem.at[1]),
        pltpu.make_async_copy(smooth, rows, sem.at[2]),
    ]
    for c in loads:
        c.start()
    start_weights(w_ref, w, w_sem)
    for c in loads:
        c.wait()
    put_targets(
        lambda k: info[1 + k // 4 : 2 + k // 4, k % 4 * B : (k % 4 + 1) * B],
        send, FAR, len(SIZES), base,
    )
    mask = (1 << BITS) - 1

    def multiply(n, carry):
        wait_weights(w_ref, w, w_sem, n)
        for j in range(0, PART, 2):
            p = n * PART + j
            one, two = jobs[0, p], jobs[0, p + 1]
            to_one = jnp.maximum((one >> (2 * BITS)) - base, 0)
            to_two = jnp.maximum((two >> (2 * BITS)) - base, 0)
            send[to_one], send[to_two] = multiply_two(
                rows[(one >> BITS) & mask],
                rows[(two >> BITS) & mask],
                w[pl.ds(p, 2)].reshape(2 * B, B),
            )
        return carry

    lax.fori_loop(0, WEIGHT_PARTS, multiply, 0)
    put_messages(send, outs, out_sem, FAR, len(SIZES), base)


def messages(first, last):
    return [
        jax.ShapeDtypeStruct((SIZES[n] + 1, F, B), jnp.float32)
        for n in range(first, last)
        for _ in range(X)
    ]


def remap_far(atmos, kappa, packed, north, south, weights):
    vmem, anywhere = (pl.BlockSpec(memory_space=m) for m in (pltpu.VMEM, pl.ANY))
    shapes = messages(0, FAR)
    smooth, meta, *outs = pl.pallas_call(
        far_kernel,
        out_shape=[
            jax.ShapeDtypeStruct((ROWS * COLS // B, F, B), jnp.float32),
            jax.ShapeDtypeStruct((META_ROWS, PAIRS), jnp.int32),
        ]
        + shapes,
        in_specs=[anywhere] * 6,
        out_specs=[anywhere, vmem] + [anywhere] * len(shapes),
        scratch_shapes=[
            pltpu.VMEM((COLS // B, F * ROWS, B), jnp.float32),
            pltpu.VMEM((ROWS, COLS), jnp.float32),
            pltpu.VMEM((1, PAIRS), jnp.int32),
            pltpu.VMEM((2, F, COLS), jnp.float32),
            pltpu.VMEM((ROWS * COLS // B, F, B), jnp.float32),
            pltpu.VMEM((1, PAIRS), jnp.int32),
            pltpu.VMEM((MESSAGES, B), jnp.int32),
            pltpu.SMEM((1, PAIRS), jnp.int32),
            pltpu.SMEM((1,), jnp.int32),
            pltpu.VMEM((PAIRS, B, B), jnp.bfloat16),
            pltpu.VMEM((STARTS[FAR], F, B), jnp.float32),
            pltpu.SemaphoreType.DMA((WEIGHT_PARTS,)),
            pltpu.SemaphoreType.DMA((len(shapes),)),
            pltpu.SemaphoreType.DMA((COLS // B + 4,)),
        ],
        compiler_params=pltpu.CompilerParams(vmem_limit_bytes=FAR_VMEM << 20),
        cost_estimate=pl.CostEstimate(flops=1 << 20, bytes_accessed=20 << 20, transcendentals=0),
    )(atmos.reshape(F * ROWS, COLS), kappa, packed, north, south, weights)
    return smooth, meta, outs


def remap_near(meta, smooth, weights):
    shapes = messages(FAR, len(SIZES))
    return pl.pallas_call(
        near_kernel,
        out_shape=shapes,
        in_specs=[pl.BlockSpec(memory_space=pl.ANY)] * 3,
        out_specs=[pl.BlockSpec(memory_space=pl.ANY)] * len(shapes),
        scratch_shapes=[
            pltpu.VMEM((META_ROWS, PAIRS), jnp.int32),
            pltpu.SMEM((1, PAIRS), jnp.int32),
            pltpu.VMEM((ROWS * COLS // B, F, B), jnp.float32),
            pltpu.VMEM((PAIRS, B, B), jnp.bfloat16),
            pltpu.VMEM((STARTS[-1] - STARTS[FAR] + 1, F, B), jnp.float32),
            pltpu.SemaphoreType.DMA((WEIGHT_PARTS,)),
            pltpu.SemaphoreType.DMA((len(shapes),)),
            pltpu.SemaphoreType.DMA((3,)),
        ],
        compiler_params=pltpu.CompilerParams(vmem_limit_bytes=NEAR_VMEM << 20),
        cost_estimate=pl.CostEstimate(flops=1 << 33, bytes_accessed=24 << 20, transcendentals=0),
    )(meta, smooth, weights)


def gather_kernel(size, a0, a1, a2, a3, out, wide, index, sem):
    for n, a in enumerate((a0, a1, a2, a3)):
        wide[n : n + 1] = a[size, 0:1].astype(jnp.int32)
        wide[X + n : X + n + 1] = a[size, 1:2].astype(jnp.int32)
    copy = pltpu.make_async_copy(wide, index, sem)
    copy.start()
    out[...] = jnp.zeros_like(out)
    copy.wait()
    for n, a in enumerate((a0, a1, a2, a3)):

        lane = (n % 2) * (B // 2)

        def add(g, carry, n=n, a=a, lane=lane):
            for j in range(8):
                out[index[n, lane + g * 8 + j]] += a[g * 8 + j]
            return carry

        lax.fori_loop(0, (index[X + n, lane] + 7) // 8, add, 0)


def gather_class(size, slots):
    return pl.pallas_call(
        lambda *refs: gather_kernel(size, *refs),
        out_shape=jax.ShapeDtypeStruct((EMPTY + 8, F, B), jnp.float32),
        in_specs=[pl.BlockSpec(memory_space=pltpu.VMEM)] * X,
        out_specs=pl.BlockSpec(memory_space=pltpu.VMEM),
        scratch_shapes=[
            pltpu.VMEM((F, B), jnp.int32),
            pltpu.SMEM((F, B), jnp.int32),
            pltpu.SemaphoreType.DMA,
        ],
        compiler_params=pltpu.CompilerParams(vmem_limit_bytes=2 << 20),
        cost_estimate=pl.CostEstimate(
            flops=1 << 32, bytes_accessed=1 << 20, transcendentals=0
        ),
    )(*slots)


def body(atmos, kappa, weights, pair_land, pair_atm, land_mask):
    tiles = X * Z
    north = lax.ppermute(atmos[:, -1, :], "tile", [(i, (i + 1) % tiles) for i in range(tiles)])
    south = lax.ppermute(atmos[:, 0, :], "tile", [((i + 1) % tiles, i) for i in range(tiles)])
    packed = (pair_land + (pair_atm << LAND_BITS)).reshape(1, PAIRS)
    smooth, meta, far = remap_far(atmos, kappa, packed, north, south, weights)
    sends = [*far, *remap_near(meta, smooth, weights)]
    sends = [sends[n * X : (n + 1) * X] for n in range(len(SIZES))]
    dense = {}
    came = None
    for n, (own, *away) in enumerate(sends):
        if came is not None:
            if n >= FAR:
                came, away = zip(*(lax.optimization_barrier(both) for both in zip(came, away)))
            dense[DISTANCES[n - 1]] = gather_class(SIZES[n - 1], [mine, *came])
        came, mine = [send_x(a, ex + 1) for ex, a in enumerate(away)], own
    dense[0] = gather_class(SIZES[-1], [mine, *came])
    half = LAND // 2
    pad = ((0, half), (0, 0), (0, 0))
    plus, minus = send_z(dense[4][:half], 1), send_z(dense[4][half:LAND], -1)
    plus, minus = jnp.pad(plus, pad), jnp.pad(minus, (pad[0][::-1], pad[1], pad[2]))
    for k in (3, 2, 1):
        plus = send_z(dense[k][:LAND] + plus, 1)
        minus = send_z(dense[k][LAND : 2 * LAND] + minus, -1)
    total = dense[0][:LAND] + plus + minus
    return total * land_mask.astype(jnp.float32)[:, None, None]


def solution(mesh):
    in_specs = (
        P("mem", "tile", None),
        P("tile", None),
        P("tile", None, None),
        P("tile"),
        P("tile"),
        P("tile"),
    )
    out_specs = P("tile", "mem", None)
    return jax.shard_map(body, mesh=mesh, in_specs=in_specs, out_specs=out_specs, check_vma=False)
```

```python
import jax
import jax.numpy as jnp
from jax import lax
from jax.experimental import pallas as pl
from jax.experimental.pallas import tpu as pltpu
from jax.sharding import PartitionSpec as P

X, Z = 4, 8
F, B = 8, 128
ROWS, COLS = 64, 1024
LAND = 128
PAIRS = 512
CAP = 32
EMPTY = 2 * LAND
GROUP = 16
PART = 32
WEIGHT_PARTS = PAIRS // PART
FAR_VMEM, NEAR_VMEM = 50, 44
DISTANCES = (4, 3, 2, 1, 0)
SIZES = (CAP, 2 * CAP, 2 * CAP, 2 * CAP, CAP)
STARTS = tuple(X * (sum(SIZES[:n]) + n) for n in range(len(SIZES) + 1))
BITS = 9
MESSAGES = X * len(SIZES)
META_ROWS = 1 + MESSAGES // 4
FAR = 2
LAND_BITS = 12


def shift(dx, dz):
    return [
        (x * Z + z, ((x + dx) % X) * Z + (z + dz) % Z) for x in range(X) for z in range(Z)
    ]


def send_x(a, dx):
    return lax.ppermute(a, "tile", shift(dx, 0))


def send_z(a, dz):
    return lax.ppermute(a, "tile", shift(0, dz))


def make_plan(packed, meta_ref, order_ref, bounds_ref, table_ref):
    land, atm = packed & ((1 << LAND_BITS) - 1), packed >> LAND_BITS
    t = lax.axis_index("tile")
    x, z = t // Z, t % Z
    owner, row = land >> 7, land & (LAND - 1)
    ex = ((owner >> 3) - x) & (X - 1)
    delta = ((owner & (Z - 1)) - z) & (Z - 1)
    dist = jnp.minimum(delta, Z - delta)
    start = jnp.zeros_like(dist)
    for n, d in enumerate(DISTANCES):
        start = jnp.where(dist == d, STARTS[n] + ex * (SIZES[n] + 1), start)
    bounds_ref[0] = jnp.sum((start < STARTS[FAR]).astype(jnp.int32))
    target = row + jnp.where(delta > 4, LAND, 0) - EMPTY

    def column(a):
        return jnp.transpose(jnp.broadcast_to(a, (F, PAIRS)))[:, 0:1]

    def total(a):
        return jnp.sum(a, axis=0, keepdims=True)

    square = (PAIRS, PAIRS)
    p_row = lax.broadcasted_iota(jnp.int32, (1, PAIRS), 1)
    earlier = lax.broadcasted_iota(jnp.int32, square, 0) < lax.broadcasted_iota(
        jnp.int32, square, 1
    )
    start_col = column(start)
    one = jnp.ones(square, jnp.int32)
    nil = jnp.zeros(square, jnp.int32)
    rank = total(jnp.where((start_col == start) & earlier, one, nil))
    place = rank + total(jnp.where(start_col < start, one, nil))
    slot = start + rank
    job = p_row + (atm << BITS) + (slot << (2 * BITS))
    meta_ref[0:1] = job
    order_ref[...] = total(jnp.where(column(place) == p_row, column(job), 0))
    slot_col, target_col = column(slot), column(target)
    lane = lax.broadcasted_iota(jnp.int32, (1, B), 1)
    for n in range(len(SIZES)):
        for m in range(X // 2):
            head = STARTS[n] + 2 * m * (SIZES[n] + 1)
            spot = jnp.where(lane < B // 2, head + lane, head + SIZES[n] + 1 + lane - B // 2)
            spot = jnp.where(lane % (B // 2) < SIZES[n], spot, -1)
            hit = total(jnp.where(slot_col == spot, target_col, 0))
            used = (hit != 0).astype(jnp.int32)
            left = jnp.sum(jnp.where(lane < B // 2, used, 0), axis=1, keepdims=True)
            right = jnp.sum(used, axis=1, keepdims=True) - left
            k = n * (X // 2) + m
            table_ref[k : k + 1] = EMPTY + hit
            table_ref[MESSAGES // 2 + k : MESSAGES // 2 + k + 1] = jnp.where(
                lane < B // 2, left, right
            )
    for k in range(MESSAGES):
        at = slice(k % 4 * B, (k % 4 + 1) * B)
        meta_ref[1 + k // 4 : 2 + k // 4, at] = table_ref[k : k + 1]


def start_weights(w_ref, w, sem):
    for n in range(WEIGHT_PARTS):
        at = pl.ds(n * PART, PART)
        pltpu.make_async_copy(w_ref.at[at], w.at[at], sem.at[n]).start()


def wait_weights(w_ref, w, sem, n):
    at = pl.ds(n * PART, PART)
    pltpu.make_async_copy(w_ref.at[at], w.at[at], sem.at[n]).wait()


def put_targets(row, send, first, last, base):
    for n in range(first, last):
        for e in range(X):
            end = STARTS[n] + (e + 1) * (SIZES[n] + 1) - 1 - base
            k = n * (X // 2) + e // 2
            send[end, 0:1] = row(k).astype(jnp.float32)
            send[end, 1:2] = row(MESSAGES // 2 + k).astype(jnp.float32)


def multiply_two(left, right, w):
    left, right = left.astype(jnp.bfloat16), right.astype(jnp.bfloat16)
    nil = jnp.zeros_like(left)
    both = jnp.concatenate(
        [jnp.concatenate([left, nil], axis=1), jnp.concatenate([nil, right], axis=1)], axis=0
    )
    out = jnp.dot(both, w, preferred_element_type=jnp.float32)
    return out[:F], out[F:]


def put_messages(send, outs, sem, first, last, base):
    copies = []
    for n in range(first, last):
        for e in range(X):
            at = STARTS[n] + e * (SIZES[n] + 1) - base
            k = len(copies)
            copies.append(
                pltpu.make_async_copy(send.at[pl.ds(at, SIZES[n] + 1)], outs[k], sem.at[k])
            )
    for c in copies:
        c.start()
    for c in copies:
        c.wait()


def far_kernel(atmos, kappa, packed, north, south, w_ref, smooth, meta, *rest):
    *outs, field, coeff, pairs, edge, rows, order, table, place, bounds, w, send = rest[:-3]
    w_sem, out_sem, sem = rest[-3:]
    per = COLS // B
    small = pltpu.make_async_copy(packed, pairs, sem.at[per])
    small.start()
    copies = [
        pltpu.make_async_copy(atmos.at[:, pl.ds(c * B, B)], field.at[c], sem.at[c])
        for c in range(per)
    ] + [
        pltpu.make_async_copy(kappa, coeff, sem.at[per + 1]),
        pltpu.make_async_copy(north, edge.at[0], sem.at[per + 2]),
        pltpu.make_async_copy(south, edge.at[1], sem.at[per + 3]),
    ]
    for c in copies:
        c.start()
    small.wait()
    for c in copies:
        c.wait()
    start_weights(w_ref, w, w_sem)
    make_plan(pairs[...], meta, order, bounds, table)
    to_smem = pltpu.make_async_copy(order, place, sem.at[per])
    to_smem.start()
    tile = lax.axis_index("tile")
    above = jnp.where(tile > 0, edge[0], 0.0)
    under = jnp.where(tile < X * Z - 1, edge[1], 0.0)

    def row(r):
        return jnp.concatenate([field[c, pl.ds(r, F, stride=ROWS), :] for c in range(per)], axis=1)

    def step(r, carry):
        prev, cur = carry
        nxt = row(jnp.minimum(r + 1, ROWS - 1))
        below = jnp.where(r < ROWS - 1, nxt, under)
        east = pltpu.roll(cur, COLS - 1, 1)
        west = pltpu.roll(cur, 1, 1)
        value = cur + coeff[pl.ds(r, 1), :] * (prev + below + east + west - 4.0 * cur)
        for c in range(per):
            rows[r * per + c] = value[:, c * B : (c + 1) * B]
        return cur, nxt

    lax.fori_loop(0, ROWS, step, (above, row(0)), unroll=4)
    save = pltpu.make_async_copy(rows, smooth, sem.at[0])
    save.start()
    put_targets(lambda k: table[k : k + 1], send, 0, FAR, 0)
    to_smem.wait()
    for n in range(WEIGHT_PARTS):
        wait_weights(w_ref, w, w_sem, n)
    mask = (1 << BITS) - 1
    high = bounds[0]

    def multiply(n, carry):
        for j in range(0, GROUP, 2):
            one = place[0, jnp.minimum(n * GROUP + j, high - 1)]
            two = place[0, jnp.minimum(n * GROUP + j + 1, high - 1)]
            send[one >> (2 * BITS)], send[two >> (2 * BITS)] = multiply_two(
                rows[(one >> BITS) & mask],
                rows[(two >> BITS) & mask],
                jnp.concatenate([w[one & mask], w[two & mask]], axis=0),
            )
        return carry

    lax.fori_loop(0, (high + GROUP - 1) // GROUP, multiply, 0)
    put_messages(send, outs, out_sem, 0, FAR, 0)
    save.wait()


def near_kernel(meta, smooth, w_ref, *rest):
    *outs, info, jobs, rows, w, send, w_sem, out_sem, sem = rest
    base = STARTS[FAR] - 1
    loads = [
        pltpu.make_async_copy(meta, info, sem.at[0]),
        pltpu.make_async_copy(meta.at[pl.ds(0, 1)], jobs, sem.at[1]),
        pltpu.make_async_copy(smooth, rows, sem.at[2]),
    ]
    for c in loads:
        c.start()
    start_weights(w_ref, w, w_sem)
    for c in loads:
        c.wait()
    put_targets(
        lambda k: info[1 + k // 4 : 2 + k // 4, k % 4 * B : (k % 4 + 1) * B],
        send, FAR, len(SIZES), base,
    )
    mask = (1 << BITS) - 1

    def multiply(n, carry):
        wait_weights(w_ref, w, w_sem, n)
        for j in range(0, PART, 2):
            p = n * PART + j
            one, two = jobs[0, p], jobs[0, p + 1]
            to_one = jnp.maximum((one >> (2 * BITS)) - base, 0)
            to_two = jnp.maximum((two >> (2 * BITS)) - base, 0)
            send[to_one], send[to_two] = multiply_two(
                rows[(one >> BITS) & mask],
                rows[(two >> BITS) & mask],
                w[pl.ds(p, 2)].reshape(2 * B, B),
            )
        return carry

    lax.fori_loop(0, WEIGHT_PARTS, multiply, 0)
    put_messages(send, outs, out_sem, FAR, len(SIZES), base)


def messages(first, last):
    return [
        jax.ShapeDtypeStruct((SIZES[n] + 1, F, B), jnp.float32)
        for n in range(first, last)
        for _ in range(X)
    ]


def remap_far(atmos, kappa, packed, north, south, weights):
    vmem, anywhere = (pl.BlockSpec(memory_space=m) for m in (pltpu.VMEM, pl.ANY))
    shapes = messages(0, FAR)
    smooth, meta, *outs = pl.pallas_call(
        far_kernel,
        out_shape=[
            jax.ShapeDtypeStruct((ROWS * COLS // B, F, B), jnp.float32),
            jax.ShapeDtypeStruct((META_ROWS, PAIRS), jnp.int32),
        ]
        + shapes,
        in_specs=[anywhere] * 6,
        out_specs=[anywhere, vmem] + [anywhere] * len(shapes),
        scratch_shapes=[
            pltpu.VMEM((COLS // B, F * ROWS, B), jnp.float32),
            pltpu.VMEM((ROWS, COLS), jnp.float32),
            pltpu.VMEM((1, PAIRS), jnp.int32),
            pltpu.VMEM((2, F, COLS), jnp.float32),
            pltpu.VMEM((ROWS * COLS // B, F, B), jnp.float32),
            pltpu.VMEM((1, PAIRS), jnp.int32),
            pltpu.VMEM((MESSAGES, B), jnp.int32),
            pltpu.SMEM((1, PAIRS), jnp.int32),
            pltpu.SMEM((1,), jnp.int32),
            pltpu.VMEM((PAIRS, B, B), jnp.bfloat16),
            pltpu.VMEM((STARTS[FAR], F, B), jnp.float32),
            pltpu.SemaphoreType.DMA((WEIGHT_PARTS,)),
            pltpu.SemaphoreType.DMA((len(shapes),)),
            pltpu.SemaphoreType.DMA((COLS // B + 4,)),
        ],
        compiler_params=pltpu.CompilerParams(vmem_limit_bytes=FAR_VMEM << 20),
        cost_estimate=pl.CostEstimate(flops=1 << 20, bytes_accessed=20 << 20, transcendentals=0),
    )(atmos.reshape(F * ROWS, COLS), kappa, packed, north, south, weights)
    return smooth, meta, outs


def remap_near(meta, smooth, weights):
    shapes = messages(FAR, len(SIZES))
    return pl.pallas_call(
        near_kernel,
        out_shape=shapes,
        in_specs=[pl.BlockSpec(memory_space=pl.ANY)] * 3,
        out_specs=[pl.BlockSpec(memory_space=pl.ANY)] * len(shapes),
        scratch_shapes=[
            pltpu.VMEM((META_ROWS, PAIRS), jnp.int32),
            pltpu.SMEM((1, PAIRS), jnp.int32),
            pltpu.VMEM((ROWS * COLS // B, F, B), jnp.float32),
            pltpu.VMEM((PAIRS, B, B), jnp.bfloat16),
            pltpu.VMEM((STARTS[-1] - STARTS[FAR] + 1, F, B), jnp.float32),
            pltpu.SemaphoreType.DMA((WEIGHT_PARTS,)),
            pltpu.SemaphoreType.DMA((len(shapes),)),
            pltpu.SemaphoreType.DMA((3,)),
        ],
        compiler_params=pltpu.CompilerParams(vmem_limit_bytes=NEAR_VMEM << 20),
        cost_estimate=pl.CostEstimate(flops=1 << 33, bytes_accessed=24 << 20, transcendentals=0),
    )(meta, smooth, weights)


def gather_kernel(size, a0, a1, a2, a3, out, wide, index, sem):
    for n, a in enumerate((a0, a1, a2, a3)):
        wide[n : n + 1] = a[size, 0:1].astype(jnp.int32)
        wide[X + n : X + n + 1] = a[size, 1:2].astype(jnp.int32)
    copy = pltpu.make_async_copy(wide, index, sem)
    copy.start()
    out[...] = jnp.zeros_like(out)
    copy.wait()
    for n, a in enumerate((a0, a1, a2, a3)):

        lane = (n % 2) * (B // 2)

        def add(g, carry, n=n, a=a, lane=lane):
            for j in range(8):
                out[index[n, lane + g * 8 + j]] += a[g * 8 + j]
            return carry

        lax.fori_loop(0, (index[X + n, lane] + 7) // 8, add, 0)


def gather_class(size, slots):
    return pl.pallas_call(
        lambda *refs: gather_kernel(size, *refs),
        out_shape=jax.ShapeDtypeStruct((EMPTY + 8, F, B), jnp.float32),
        in_specs=[pl.BlockSpec(memory_space=pltpu.VMEM)] * X,
        out_specs=pl.BlockSpec(memory_space=pltpu.VMEM),
        scratch_shapes=[
            pltpu.VMEM((F, B), jnp.int32),
            pltpu.SMEM((F, B), jnp.int32),
            pltpu.SemaphoreType.DMA,
        ],
        compiler_params=pltpu.CompilerParams(vmem_limit_bytes=2 << 20),
        cost_estimate=pl.CostEstimate(
            flops=1 << 32, bytes_accessed=1 << 20, transcendentals=0
        ),
    )(*slots)


def body(atmos, kappa, weights, pair_land, pair_atm, land_mask):
    tiles = X * Z
    north = lax.ppermute(atmos[:, -1, :], "tile", [(i, (i + 1) % tiles) for i in range(tiles)])
    south = lax.ppermute(atmos[:, 0, :], "tile", [((i + 1) % tiles, i) for i in range(tiles)])
    packed = (pair_land + (pair_atm << LAND_BITS)).reshape(1, PAIRS)
    smooth, meta, far = remap_far(atmos, kappa, packed, north, south, weights)
    sends = [*far, *remap_near(meta, smooth, weights)]
    sends = [sends[n * X : (n + 1) * X] for n in range(len(SIZES))]
    dense = {}
    came = None
    for n, (own, *away) in enumerate(sends):
        if came is not None:
            if n >= FAR:
                came, away = zip(*(lax.optimization_barrier(both) for both in zip(came, away)))
            dense[DISTANCES[n - 1]] = gather_class(SIZES[n - 1], [mine, *came])
        came, mine = [send_x(a, ex + 1) for ex, a in enumerate(away)], own
    dense[0] = gather_class(SIZES[-1], [mine, *came])
    half = LAND // 2
    pad = ((0, half), (0, 0), (0, 0))
    plus, minus = send_z(dense[4][:half], 1), send_z(dense[4][half:LAND], -1)
    plus, minus = jnp.pad(plus, pad), jnp.pad(minus, (pad[0][::-1], pad[1], pad[2]))
    for k in (3, 2, 1):
        own = dense[k]
        up = own[:LAND] + plus
        if k in (2,):
            own, up = lax.optimization_barrier((own, up))
        down = own[LAND : 2 * LAND] + minus
        plus, minus = send_z(up, 1), send_z(down, -1)
    total = dense[0][:LAND] + plus + minus
    return total * land_mask.astype(jnp.float32)[:, None, None]


def solution(mesh):
    in_specs = (
        P("mem", "tile", None),
        P("tile", None),
        P("tile", None, None),
        P("tile"),
        P("tile"),
        P("tile"),
    )
    out_specs = P("tile", "mem", None)
    return jax.shard_map(body, mesh=mesh, in_specs=in_specs, out_specs=out_specs, check_vma=False)
```
